32 devices in a mesh: pipe: 2 (over core), obs: 4 (over y, x), patch: 4 (over z).
Axes of the slice: x: 2, y: 2, z: 4, core: 2. Of those that a mesh axis runs over, the one named last changes fastest.
Arguments:
- patch_tokens: bfloat16 [2048, 2048], P('patch', 'obs'), may hold values from -40 to 40
- obs_tokens: bfloat16 [1024, 2048], P('patch', 'obs'), may hold values from -40 to 40
- footprint: int32 [16, 4], P('patch'), may hold values from 0 to 7, as said below
- list_counts: int32 [16], P('patch'), may hold values from 1 to 4
- footprint_bias: float32 [16, 4], P('patch'), may hold values from -4 to 290
- w_query: bfloat16 [2, 2048, 2048], P('pipe', None, 'obs'), may hold values from -0.125 to 0.125
- w_key: bfloat16 [2, 2048, 2048], P('pipe', None, 'obs'), may hold values from -0.125 to 0.125
- w_value: bfloat16 [2, 2048, 2048], P('pipe', None, 'obs'), may hold values from -0.125 to 0.125
- w_out: bfloat16 [2, 2048, 2048], P('pipe', 'obs'), may hold values from -0.125 to 0.125
- patch_gain: float32 [2, 2048], P('pipe'), may hold values from 0.1 to 1.9
- obs_gain: float32 [2, 2048], P('pipe'), may hold values from 0.1 to 1.9
Outputs:
- sections: bfloat16 [2, 2048, 2048], P('pipe', 'patch', 'obs')
The draws below stay inside these ranges and needn't reach their ends.
Inputs may be any that keep to these rules, and one draw needn't show every extreme that they name: `footprint`: entries are global observation block indices. In each row the first list_counts entries (the live ones) are distinct, the rest are to be ignored. For a device along patch and any device along patch, all live entries of the first device's rows that lie in the second device's range of 2 blocks name one and the same block.
All inputs are finite; a program needn't handle non-finite values.
Results may differ from the reference program's by a relative error of at most 0.012.
Values may be sent and summed in bfloat16 or wider, within the bound.
A program may use at most 64 MiB of HBM per device.

```python
import math
import jax
import jax.numpy as jnp
from jax import lax

D = 2048
HEADS = 16
HS = 128
BLK = 128
SEGMENTS = 2
GROUPS = 4
MAXL = 4
P_SIZE = 2048
NOBS = 1024
PBLK = 16
NOBLK = 8
PBLK_DEV = 4
OBLK_DEV = 2


def token_field(key, row_count, col_count):
    base_field = jax.random.truncated_normal(jax.random.fold_in(key, 1), -4.0, 4.0, (row_count, col_count), jnp.float32)
    row_scale = jnp.exp(jax.random.uniform(jax.random.fold_in(key, 2), (row_count, 1), jnp.float32, math.log(0.3), math.log(3.0)))
    col_scale = jnp.exp(jax.random.uniform(jax.random.fold_in(key, 3), (1, col_count), jnp.float32, math.log(0.5), math.log(2.0)))
    return (base_field * row_scale * col_scale).astype(jnp.bfloat16)


def draw_patch_tokens(key, part):
    return token_field(jax.random.fold_in(key, 101), P_SIZE, D)


def draw_obs_tokens(key, part):
    return token_field(jax.random.fold_in(key, 202), NOBS, D)


def footprint_parts(key):
    device_count = PBLK // PBLK_DEV
    picked = jax.random.randint(jax.random.fold_in(key, 11), (device_count, device_count), 0, OBLK_DEV)
    block_keys = jax.random.split(jax.random.fold_in(key, 12), PBLK)
    orders = jax.vmap(lambda one_key: jax.random.permutation(one_key, device_count))(block_keys)
    chosen = orders[:, :MAXL].astype(jnp.int32)
    owners = (jnp.arange(PBLK) // PBLK_DEV).astype(jnp.int32)
    entries = chosen * OBLK_DEV + picked[owners[:, None], chosen]
    counts = jax.random.randint(jax.random.fold_in(key, 13), (PBLK,), 1, MAXL + 1)
    full_at = jax.random.randint(jax.random.fold_in(key, 14), (), 0, PBLK)
    counts = jnp.where(jnp.arange(PBLK) == full_at, MAXL, counts)
    return (entries.astype(jnp.int32), counts.astype(jnp.int32))


def draw_footprint(key, part):
    entries, counts = footprint_parts(jax.random.fold_in(key, 303))
    return entries


def draw_list_counts(key, part):
    entries, counts = footprint_parts(jax.random.fold_in(key, 303))
    return counts


def draw_footprint_bias(key, part):
    values = jax.random.uniform(jax.random.fold_in(key, 32), (PBLK, MAXL), jnp.float32, -2.0, 2.0)
    return values


def level_of(own_key, shape, cuts, low, top_value):
    loudness = 1.0
    for position, shards_of in cuts:
        steps = jax.random.uniform(jax.random.fold_in(jax.random.fold_in(own_key, 6), position), (shards_of,), jnp.float32, low / len(cuts), top_value / len(cuts))
        loudness = loudness * jnp.repeat(jnp.exp(steps), shape[position] // shards_of).reshape((-1,) + (1,) * (len(shape) - 1 - position))
    return loudness


def centred(stream_key, shape, scale, bound, shards=(), dtype=jnp.bfloat16):
    values = scale * jax.random.normal(stream_key, shape, jnp.float32)
    if shards:
        values = values * level_of(stream_key, shape, shards, -0.22, 0.18)
    return jnp.clip(values, -bound, bound).astype(dtype)


def setup_inputs(seed: int = 0) -> dict:
    keys = jax.random.split(jax.random.key(seed), 12)
    patch_tokens = draw_patch_tokens(jax.random.fold_in(keys[11], 71), 0)
    obs_tokens = draw_obs_tokens(jax.random.fold_in(keys[11], 71), 0)
    footprint = draw_footprint(jax.random.fold_in(keys[11], 71), 0)
    list_counts = draw_list_counts(jax.random.fold_in(keys[11], 71), 0)
    footprint_bias = draw_footprint_bias(jax.random.fold_in(keys[11], 71), 0)
    w_query = centred(keys[5], (SEGMENTS, D, HEADS * HS), D ** -0.5, 0.125, ((0, 2), (2, 4)))
    w_key = centred(keys[6], (SEGMENTS, D, HEADS * HS), D ** -0.5, 0.125, ((0, 2), (2, 4)))
    w_value = centred(keys[7], (SEGMENTS, D, HEADS * HS), D ** -0.5, 0.125, ((0, 2), (2, 4)))
    w_out = centred(keys[8], (SEGMENTS, HEADS * HS, D), (HEADS * HS) ** -0.5, 0.125, ((0, 2), (1, 4)))
    patch_gain = jnp.clip(1.0 + 0.18 * jax.random.normal(keys[9], (SEGMENTS, D), jnp.float32), 0.1, 1.9)
    obs_gain = jnp.clip(1.0 + 0.18 * jax.random.normal(keys[10], (SEGMENTS, D), jnp.float32), 0.1, 1.9)
    return dict(patch_tokens=patch_tokens, obs_tokens=obs_tokens, footprint=footprint, list_counts=list_counts, footprint_bias=footprint_bias, w_query=w_query, w_key=w_key, w_value=w_value, w_out=w_out, patch_gain=patch_gain, obs_gain=obs_gain)


def rms_round(values, gain):
    widened = values.astype(jnp.float32)
    scaled = widened * lax.rsqrt(lax.optimization_barrier(jnp.mean(widened * widened, axis=-1, keepdims=True)) + 1e-05)
    return (scaled * gain.astype(jnp.float32)).astype(jnp.bfloat16)

def reference(patch_tokens, obs_tokens, footprint, list_counts, footprint_bias, w_query, w_key, w_value, w_out, patch_gain, obs_gain):
    full_width = HEADS * HS
    group_width = full_width // GROUPS
    current = patch_tokens
    results = []
    for section in range(SEGMENTS):
        obs_normed = rms_round(obs_tokens, obs_gain[section])
        key_rows = jnp.dot(obs_normed, w_key[section], preferred_element_type=jnp.float32).astype(jnp.bfloat16)
        value_rows = jnp.dot(obs_normed, w_value[section], preferred_element_type=jnp.float32).astype(jnp.bfloat16)
        key_rows = lax.optimization_barrier(key_rows).reshape(NOBLK, BLK, HEADS, HS)
        value_rows = lax.optimization_barrier(value_rows).reshape(NOBLK, BLK, HEADS, HS)
        patch_normed = rms_round(current, patch_gain[section])
        queries = (jnp.dot(patch_normed, w_query[section], preferred_element_type=jnp.float32) * HS ** (-0.5)).astype(jnp.bfloat16)
        queries = lax.optimization_barrier(queries).reshape(PBLK, BLK, HEADS, HS)

        def one_block(items):
            query_block, listed, count_live, bias_row = items
            key_block = key_rows[listed].reshape(MAXL * BLK, HEADS, HS).astype(jnp.float32)
            value_block = value_rows[listed].reshape(MAXL * BLK, HEADS, HS).astype(jnp.float32)
            scores = jnp.einsum('qhd,khd->hqk', query_block.astype(jnp.float32), key_block)
            alive = jnp.repeat(jnp.arange(MAXL) < count_live, BLK)
            added = jnp.repeat(bias_row.astype(jnp.float32), BLK)
            scores = jnp.where(alive[None, None, :], scores + added[None, None, :], -1e+30)
            row_max = lax.optimization_barrier(jnp.max(scores, axis=-1, keepdims=True))
            weights = jnp.exp(scores - row_max)
            weights = (weights / lax.optimization_barrier(jnp.sum(weights, axis=-1, keepdims=True))).astype(jnp.bfloat16)
            weights = lax.optimization_barrier(weights).astype(jnp.float32)
            context = jnp.einsum('hqk,khd->qhd', weights, value_block).astype(jnp.bfloat16)
            return context.reshape(BLK, full_width)
        context = lax.map(one_block, (queries, footprint, list_counts, footprint_bias)).reshape(P_SIZE, full_width)
        head_total = jnp.zeros((P_SIZE, D), jnp.float32)
        for group in range(GROUPS):
            lower = group * group_width
            head_part = jnp.dot(context[:, lower:lower + group_width], w_out[section][lower:lower + group_width], preferred_element_type=jnp.float32).astype(jnp.bfloat16)
            head_part = lax.optimization_barrier(head_part)
            head_total = head_total + head_part.astype(jnp.float32)
        current = (current.astype(jnp.float32) + head_total).astype(jnp.bfloat16)
        results.append(current)
    return jnp.stack(results)
```

```python
import functools
import jax
import jax.numpy as jnp
from jax import lax
from jax.experimental import pallas as pl
from jax.experimental.pallas import tpu as pltpu
from jax.sharding import PartitionSpec as P

HS = 128
BLK = 128
HALF = BLK // 2
EPS = 1e-05
NEG = -1e30
F32 = jnp.float32
BF16 = jnp.bfloat16


def rms_round(values, gain):
    widened = values.astype(F32)
    scaled = widened * lax.rsqrt(jnp.mean(widened * widened, axis=-1, keepdims=True) + EPS)
    return (scaled * gain).astype(BF16)


def remote(src, dst, send_sem, recv_sem, pipe, obs, patch):
    return pltpu.make_async_remote_copy(
        src_ref=src,
        dst_ref=dst,
        send_sem=send_sem,
        recv_sem=recv_sem,
        device_id={"pipe": pipe, "obs": obs, "patch": patch},
        device_id_type=pl.DeviceIdType.MESH,
    )


def kernel(
    n_obs,
    n_patch,
    patch_hbm,
    obs_hbm,
    footprint,
    counts,
    slot_bias,
    wq_hbm,
    wk_hbm,
    wv_hbm,
    wo_hbm,
    patch_gain,
    obs_gain,
    out,
    wq,
    wk,
    wv,
    wo,
    xbuf,
    zbuf,
    sel,
    ofull,
    keys,
    vals,
    queries,
    context,
    pbuf,
    rbuf,
    x1,
    bias,
    w_sem,
    own_sem,
    z_send,
    z_recv,
    o_send,
    o_recv,
    f_send,
    x_send,
    x_recv,
    r_send,
    r_recv,
):
    p = lax.axis_index("pipe")
    o = lax.axis_index("obs")
    z = lax.axis_index("patch")
    rows_total, feat = out.shape
    micro = rows_total // BLK
    heads = wq.shape[1] // HS
    range_blocks = zbuf.shape[1]
    half_rows = sel.shape[0]
    peers = [lax.rem(o + k, n_obs) for k in range(n_obs)]
    zpeers = [lax.rem(z + k, n_patch) for k in range(n_patch)]

    def cols(index):
        return pl.ds(pl.multiple_of(index * feat, feat), feat)

    def rows(index):
        return pl.ds(pl.multiple_of(index * BLK, BLK), BLK)

    barrier = pltpu.get_barrier_semaphore()
    for k in range(n_obs):
        pl.semaphore_signal(
            barrier, inc=1, device_id={"pipe": 1 - p, "obs": peers[k], "patch": z},
            device_id_type=pl.DeviceIdType.MESH,
        )
        if k:
            pl.semaphore_signal(
                barrier, inc=1, device_id={"pipe": p, "obs": peers[k], "patch": z},
                device_id_type=pl.DeviceIdType.MESH,
            )
    for k in range(1, n_patch):
        pl.semaphore_signal(
            barrier, inc=1, device_id={"pipe": p, "obs": o, "patch": zpeers[k]},
            device_id_type=pl.DeviceIdType.MESH,
        )
    own_obs = pltpu.make_async_copy(obs_hbm.at[:, p], zbuf.at[z], own_sem.at[0])
    own_obs.start()
    own_patch = pltpu.make_async_copy(patch_hbm, xbuf.at[:, cols(o)], own_sem.at[1])

    @pl.when(p == 0)
    def _():
        own_patch.start()

    w_copies = [
        pltpu.make_async_copy(src, dst, w_sem.at[i])
        for i, (src, dst) in enumerate(
            ((wq_hbm, wq), (wk_hbm, wk), (wv_hbm, wv), (wo_hbm, wo))
        )
    ]
    for copy in w_copies:
        copy.start()
    pl.semaphore_wait(barrier, 2 * n_obs - 1 + n_patch - 1)

    def z_copy(k):
        return remote(
            obs_hbm.at[:, p], zbuf.at[z], z_send.at[k], z_recv.at[z], p, o, zpeers[k]
        )

    def patch_copy(m, k):
        return remote(
            patch_hbm.at[rows(m), :], xbuf.at[rows(m), cols(o)],
            x_send.at[m, k], x_recv.at[m, o], 0, peers[k], z,
        )

    for k in range(1, n_patch):
        z_copy(k).start()

    @pl.when(p == 0)
    def _():
        @pl.loop(0, micro)
        def _(m):
            for k in range(1, n_obs):
                patch_copy(m, k).start()

    listed = footprint[...].astype(F32)
    slots = lax.broadcasted_iota(jnp.int32, listed.shape, 1)
    alive = slots < counts[...]
    added = slot_bias[...]
    col = lax.broadcasted_iota(jnp.int32, bias.shape, 1)
    source = lax.rem(lax.div(col, HALF), n_patch)
    full_bias = jnp.full(bias.shape, NEG, F32)
    wanted = []
    for zz in range(n_patch):
        low = zz * range_blocks
        match = alive & (listed >= float(low)) & (listed < float(low + range_blocks))
        one = jnp.max(jnp.where(match, added, NEG), axis=1, keepdims=True)
        full_bias = jnp.where(source == zz, one, full_bias)
        which = jnp.max(jnp.where(match, listed - float(low), 0.0), axis=1, keepdims=True)
        wanted.append(jnp.max(which, axis=0, keepdims=True))
    bias[...] = full_bias

    own_obs.wait()
    for k in range(1, n_patch):
        remote(
            obs_hbm.at[:, p], zbuf.at[zpeers[k]], z_send.at[k], z_recv.at[zpeers[k]],
            p, o, zpeers[k],
        ).wait_recv()
    for zz in range(n_patch):
        picked = zbuf[zz, 0].astype(F32)
        which = jnp.broadcast_to(wanted[zz], picked.shape)
        for k in range(1, range_blocks):
            picked = jnp.where(which == float(k), zbuf[zz, k].astype(F32), picked)
        sel[zz * HALF : (zz + 1) * HALF, :] = picked.astype(BF16)

    def sel_copy(k):
        if k == 0:
            return remote(
                sel, ofull.at[p, :, cols(o)], o_send.at[0], o_recv.at[p, o], 1 - p, o, z
            )
        return remote(
            sel, ofull.at[p, :, cols(o)], o_send.at[k], o_recv.at[p, o], p, peers[k], z
        )

    def forward(k):
        slab = ofull.at[p, :, cols(peers[k])]
        return remote(
            slab, slab, f_send.at[k], o_recv.at[p, peers[k]], 1 - p, o, z
        )

    for k in range(1, n_obs):
        sel_copy(k).start()
    sel_copy(0).start()
    own_sel = pltpu.make_async_copy(sel, ofull.at[p, :, cols(o)], own_sem.at[2])
    own_sel.start()

    w_copies[0].wait()
    score_scale = HS ** (-0.5)

    def project(m):
        for k in range(1, n_obs):
            remote(
                patch_hbm.at[rows(m), :], xbuf.at[rows(m), cols(peers[k])],
                x_send.at[m, k], x_recv.at[m, peers[k]], 0, peers[k], z,
            ).wait_recv()
        normed = rms_round(xbuf[rows(m), :], patch_gain[...])
        queries[rows(m), :] = (
            jnp.dot(normed, wq[...], preferred_element_type=F32) * score_scale
        ).astype(BF16)

    @pl.when(p == 0)
    def _():
        own_patch.wait()

        @pl.loop(0, micro)
        def _(m):
            project(m)

    for k in range(1, n_obs):
        slab = ofull.at[p, :, cols(peers[k])]
        remote(sel, slab, o_send.at[k], o_recv.at[p, peers[k]], p, peers[k], z).wait_recv()
        forward(k).start()
    own_sel.wait()
    for k in range(n_obs):
        slab = ofull.at[1 - p, :, cols(peers[k])]
        remote(
            slab, slab, f_send.at[k], o_recv.at[1 - p, peers[k]], 1 - p, o, z
        ).wait_recv()

    w_copies[1].wait()
    w_copies[2].wait()

    @pl.loop(0, 2)
    def _(h):
        normed = rms_round(ofull[h], obs_gain[...])
        here = pl.ds(pl.multiple_of(h * half_rows, half_rows), half_rows)
        keys[here, :] = jnp.dot(normed, wk[...], preferred_element_type=F32).astype(BF16)
        vals[here, :] = jnp.dot(normed, wv[...], preferred_element_type=F32).astype(BF16)

    w_copies[3].wait()

    def piece_copy(m, k):
        return remote(
            pbuf.at[peers[k], rows(m), :], rbuf.at[o, rows(m), :],
            r_send.at[m, k], r_recv.at[m, o], p, peers[k], z,
        )

    def x1_copy(m, k):
        return remote(
            x1.at[rows(m), :], xbuf.at[rows(m), cols(o)],
            x_send.at[micro + m, k], x_recv.at[m, o], 1, peers[k], z,
        )

    def attend(m):
        row_bias = bias[pl.ds(m, 1), :]
        for h in range(heads):
            head = slice(h * HS, (h + 1) * HS)
            scores = lax.dot_general(
                queries[rows(m), head], keys[:, head], (((1,), (1,)), ((), ())),
                preferred_element_type=F32,
            )
            scores = scores + row_bias
            weights = jnp.exp(scores - jnp.max(scores, axis=-1, keepdims=True))
            total = jnp.sum(weights, axis=-1, keepdims=True)
            mixed = jnp.dot(weights.astype(BF16), vals[:, head], preferred_element_type=F32)
            context[:, head] = (mixed / total).astype(BF16)
        for k in list(range(1, n_obs)) + [0]:
            pbuf[peers[k], rows(m), :] = jnp.dot(
                context[...], wo[:, cols(peers[k])], preferred_element_type=F32
            ).astype(BF16)
            if k:
                piece_copy(m, k).start()

    def finish(m):
        for k in range(1, n_obs):
            remote(
                pbuf.at[peers[k], rows(m), :], rbuf.at[peers[k], rows(m), :],
                r_send.at[m, k], r_recv.at[m, peers[k]], p, peers[k], z,
            ).wait_recv()
        head_total = pbuf[o, rows(m), :].astype(F32)
        for k in range(1, n_obs):
            head_total = head_total + rbuf[peers[k], rows(m), :].astype(F32)
        result = (xbuf[rows(m), cols(o)].astype(F32) + head_total).astype(BF16)
        out[rows(m), :] = result

        @pl.when(p == 0)
        def _():
            x1[rows(m), :] = result
            for k in range(n_obs):
                x1_copy(m, (k + 1) % n_obs).start()

    @pl.loop(0, micro + 1)
    def _(t):
        @pl.when(t < micro)
        def _():
            @pl.when(p == 1)
            def _():
                remote(
                    x1.at[rows(t), :], xbuf.at[rows(t), cols(o)],
                    x_send.at[t, 0], x_recv.at[t, o], 0, o, z,
                ).wait_recv()
                project(t)

            attend(t)

        @pl.when(t > 0)
        def _():
            finish(t - 1)

    for k in range(1, n_patch):
        z_copy(k).wait_send()
    for k in range(n_obs):
        sel_copy(k).wait_send()
        if k:
            forward(k).wait_send()

    @pl.loop(0, micro)
    def _(m):
        for k in range(1, n_obs):
            piece_copy(m, k).wait_send()

        @pl.when(p == 0)
        def _():
            for k in range(1, n_obs):
                patch_copy(m, k).wait_send()
            for k in range(n_obs):
                x1_copy(m, k).wait_send()


def on_device(
    n_obs,
    n_patch,
    patch_tokens,
    obs_tokens,
    footprint,
    list_counts,
    footprint_bias,
    w_query,
    w_key,
    w_value,
    w_out,
    patch_gain,
    obs_gain,
):
    row_count, feat = patch_tokens.shape
    width = feat * n_obs
    head_width = w_query.shape[2]
    range_blocks = obs_tokens.shape[0] // BLK
    micro = row_count // BLK
    half_rows = n_patch * HALF
    anywhere = pl.BlockSpec(memory_space=pl.ANY)
    vmem = pl.BlockSpec(memory_space=pltpu.VMEM)
    dma = pltpu.SemaphoreType.DMA
    result = pl.pallas_call(
        functools.partial(kernel, n_obs, n_patch),
        out_shape=jax.ShapeDtypeStruct((row_count, feat), BF16),
        in_specs=[anywhere, anywhere, vmem, vmem, vmem] + [anywhere] * 4 + [vmem, vmem],
        out_specs=vmem,
        scratch_shapes=[
            pltpu.VMEM((width, head_width), BF16),
            pltpu.VMEM((width, head_width), BF16),
            pltpu.VMEM((width, head_width), BF16),
            pltpu.VMEM((head_width, width), BF16),
            pltpu.VMEM((row_count, width), BF16),
            pltpu.VMEM((n_patch, range_blocks, HALF, feat), BF16),
            pltpu.VMEM((half_rows, feat), BF16),
            pltpu.VMEM((2, half_rows, width), BF16),
            pltpu.VMEM((2 * half_rows, head_width), BF16),
            pltpu.VMEM((2 * half_rows, head_width), BF16),
            pltpu.VMEM((row_count, head_width), BF16),
            pltpu.VMEM((BLK, head_width), BF16),
            pltpu.VMEM((n_obs, row_count, feat), BF16),
            pltpu.VMEM((n_obs, row_count, feat), BF16),
            pltpu.VMEM((row_count, feat), BF16),
            pltpu.VMEM((micro, 2 * half_rows), F32),
            dma((4,)),
            dma((3,)),
            dma((n_patch,)),
            dma((n_patch,)),
            dma((n_obs,)),
            dma((2, n_obs)),
            dma((n_obs,)),
            dma((2 * micro, n_obs)),
            dma((micro, n_obs)),
            dma((micro, n_obs)),
            dma((micro, n_obs)),
        ],
        compiler_params=pltpu.CompilerParams(
            collective_id=0, has_side_effects=True, vmem_limit_bytes=44 * 1024 * 1024
        ),
    )(
        patch_tokens,
        obs_tokens.reshape(range_blocks, 2, HALF, feat),
        footprint,
        list_counts[:, None],
        footprint_bias,
        w_query[0],
        w_key[0],
        w_value[0],
        w_out[0],
        patch_gain,
        obs_gain,
    )
    return result[None]


def solution(mesh):
    in_specs = (
        P("patch", "obs"),
        P("patch", "obs"),
        P("patch", None),
        P("patch"),
        P("patch", None),
        P("pipe", None, "obs"),
        P("pipe", None, "obs"),
        P("pipe", None, "obs"),
        P("pipe", "obs", None),
        P("pipe", None),
        P("pipe", None),
    )
    out_specs = P("pipe", "patch", "obs")
    return jax.shard_map(
        functools.partial(on_device, mesh.shape["obs"], mesh.shape["patch"]),
        mesh=mesh, in_specs=in_specs, out_specs=out_specs, check_vma=False,
    )
```

```python
import functools
import jax
import jax.numpy as jnp
from jax import lax
from jax.experimental import pallas as pl
from jax.experimental.pallas import tpu as pltpu
from jax.sharding import PartitionSpec as P

HS = 128
BLK = 128
HALF = BLK // 2
EPS = 1e-05
NEG = -1e30
F32 = jnp.float32
BF16 = jnp.bfloat16


def rms_round(values, gain):
    widened = values.astype(F32)
    scaled = widened * lax.rsqrt(jnp.mean(widened * widened, axis=-1, keepdims=True) + EPS)
    return (scaled * gain).astype(BF16)


def remote(src, dst, send_sem, recv_sem, pipe, obs, patch):
    return pltpu.make_async_remote_copy(
        src_ref=src,
        dst_ref=dst,
        send_sem=send_sem,
        recv_sem=recv_sem,
        device_id={"pipe": pipe, "obs": obs, "patch": patch},
        device_id_type=pl.DeviceIdType.MESH,
    )


def kernel(
    n_obs,
    n_patch,
    patch_hbm,
    obs_hbm,
    footprint_hbm,
    counts,
    slot_bias_hbm,
    wq_hbm,
    wk_hbm,
    wv_hbm,
    wo_hbm,
    patch_gain_hbm,
    obs_gain_hbm,
    out,
    footprint,
    slot_bias,
    patch_gain,
    obs_gain,
    wq,
    wk,
    wv,
    wo,
    xbuf,
    obs_own,
    zout,
    wish,
    asked,
    sel,
    ofull,
    keys,
    vals,
    queries,
    context,
    pbuf,
    rbuf,
    x1,
    bias,
    w_sem,
    own_sem,
    a_send,
    a_recv,
    z_send,
    z_recv,
    o_send,
    o_recv,
    f_send,
    x_send,
    x_recv,
    r_send,
    r_recv,
):
    p = lax.axis_index("pipe")
    o = lax.axis_index("obs")
    z = lax.axis_index("patch")
    rows_total, feat = out.shape
    micro = rows_total // BLK
    heads = wq.shape[1] // HS
    range_blocks = obs_own.shape[0]
    half_rows = sel.shape[0]
    peers = [lax.rem(o + k, n_obs) for k in range(n_obs)]
    zpeers = [lax.rem(z + k, n_patch) for k in range(n_patch)]

    def cols(index):
        return pl.ds(pl.multiple_of(index * feat, feat), feat)

    def rows(index):
        return pl.ds(pl.multiple_of(index * BLK, BLK), BLK)

    barrier = pltpu.get_barrier_semaphore()
    for k in range(n_obs):
        pl.semaphore_signal(
            barrier, inc=1, device_id={"pipe": 1 - p, "obs": peers[k], "patch": z},
            device_id_type=pl.DeviceIdType.MESH,
        )
        if k:
            pl.semaphore_signal(
                barrier, inc=1, device_id={"pipe": p, "obs": peers[k], "patch": z},
                device_id_type=pl.DeviceIdType.MESH,
            )
    for k in range(1, n_patch):
        pl.semaphore_signal(
            barrier, inc=1, device_id={"pipe": p, "obs": o, "patch": zpeers[k]},
            device_id_type=pl.DeviceIdType.MESH,
        )
    small_copies = [
        pltpu.make_async_copy(src, dst, w_sem.at[4 + i])
        for i, (src, dst) in enumerate(
            (
                (footprint_hbm, footprint),
                (slot_bias_hbm, slot_bias),
                (patch_gain_hbm, patch_gain),
                (obs_gain_hbm, obs_gain),
            )
        )
    ]
    for copy in small_copies:
        copy.start()
    own_obs = pltpu.make_async_copy(obs_hbm.at[:, p], obs_own, own_sem.at[0])
    own_obs.start()
    own_patch = pltpu.make_async_copy(patch_hbm, xbuf.at[:, cols(o)], own_sem.at[1])

    @pl.when(p == 0)
    def _():
        own_patch.start()

    w_copies = [
        pltpu.make_async_copy(src, dst, w_sem.at[i])
        for i, (src, dst) in enumerate(
            ((wq_hbm, wq), (wk_hbm, wk), (wv_hbm, wv), (wo_hbm, wo))
        )
    ]
    for copy in w_copies:
        copy.start()
    small_copies[0].wait()
    small_copies[1].wait()
    listed = footprint[...].astype(F32)
    slots = lax.broadcasted_iota(jnp.int32, listed.shape, 1)
    row = lax.broadcasted_iota(jnp.int32, listed.shape, 0)
    live = jnp.zeros(listed.shape, jnp.int32)
    for b in range(listed.shape[0]):
        live = jnp.where(row == b, counts[b], live)
    alive = slots < live
    added = slot_bias[...]
    col = lax.broadcasted_iota(jnp.int32, bias.shape, 1)
    source = lax.rem(lax.div(col, HALF), n_patch)
    full_bias = jnp.full(bias.shape, NEG, F32)
    for zz in range(n_patch):
        low = zz * range_blocks
        match = alive & (listed >= float(low)) & (listed < float(low + range_blocks))
        one = jnp.max(jnp.where(match, added, NEG), axis=1, keepdims=True)
        full_bias = jnp.where(source == zz, one, full_bias)
        which = jnp.max(jnp.where(match, listed - float(low), 0.0), axis=1, keepdims=True)
        wish[zz] = jnp.broadcast_to(jnp.max(which, axis=0, keepdims=True), wish.shape[1:])
    bias[...] = full_bias

    pl.semaphore_wait(barrier, 2 * n_obs - 1 + n_patch - 1)

    def wish_copy(k):
        return remote(
            wish.at[zpeers[k]], asked.at[z], a_send.at[k], a_recv.at[z], p, o, zpeers[k]
        )

    def z_place(index):
        return pl.ds(pl.multiple_of(index * HALF, HALF), HALF)

    def z_copy(k):
        return remote(
            zout.at[k], sel.at[z_place(z), :], z_send.at[k], z_recv.at[z], p, o, zpeers[k]
        )

    def patch_copy(m, k):
        return remote(
            patch_hbm.at[rows(m), :], xbuf.at[rows(m), cols(o)],
            x_send.at[m, k], x_recv.at[m, o], 0, peers[k], z,
        )

    def pick(which):
        which = jnp.broadcast_to(which[0:1, 0:1], obs_own.shape[1:])
        picked = obs_own[0].astype(F32)
        for k in range(1, range_blocks):
            picked = jnp.where(which == float(k), obs_own[k].astype(F32), picked)
        return picked.astype(BF16)

    early = micro - 1
    for k in range(1, n_patch):
        wish_copy(k).start()

    @pl.when(p == 0)
    def _():
        @pl.loop(0, early)
        def _(m):
            for k in range(1, n_obs):
                patch_copy(m, k).start()

    own_obs.wait()
    sel[z_place(z), :] = pick(wish[z])
    for k in range(1, n_patch):
        remote(
            wish.at[zpeers[k]], asked.at[zpeers[k]], a_send.at[k], a_recv.at[zpeers[k]],
            p, o, zpeers[k],
        ).wait_recv()
        zout[k] = pick(asked[zpeers[k]])
        z_copy(k).start()
    for k in range(1, n_patch):
        remote(
            zout.at[k], sel.at[z_place(zpeers[k]), :], z_send.at[k], z_recv.at[zpeers[k]],
            p, o, zpeers[k],
        ).wait_recv()

    def sel_copy(k):
        if k == 0:
            return remote(
                sel, ofull.at[p, :, cols(o)], o_send.at[0], o_recv.at[p, o], 1 - p, o, z
            )
        return remote(
            sel, ofull.at[p, :, cols(o)], o_send.at[k], o_recv.at[p, o], p, peers[k], z
        )

    def forward(k):
        slab = ofull.at[p, :, cols(peers[k])]
        return remote(
            slab, slab, f_send.at[k], o_recv.at[p, peers[k]], 1 - p, o, z
        )

    for k in range(1, n_obs):
        sel_copy(k).start()
    sel_copy(0).start()
    own_sel = pltpu.make_async_copy(sel, ofull.at[p, :, cols(o)], own_sem.at[2])
    own_sel.start()

    @pl.when(p == 0)
    def _():
        @pl.loop(early, micro)
        def _(m):
            for k in range(1, n_obs):
                patch_copy(m, k).start()


    w_copies[0].wait()
    small_copies[2].wait()
    small_copies[3].wait()
    score_scale = HS ** (-0.5)

    def project(m):
        for k in range(1, n_obs):
            remote(
                patch_hbm.at[rows(m), :], xbuf.at[rows(m), cols(peers[k])],
                x_send.at[m, k], x_recv.at[m, peers[k]], 0, peers[k], z,
            ).wait_recv()
        normed = rms_round(xbuf[rows(m), :], patch_gain[...])
        queries[rows(m), :] = (
            jnp.dot(normed, wq[...], preferred_element_type=F32) * score_scale
        ).astype(BF16)

    @pl.when(p == 0)
    def _():
        own_patch.wait()

        @pl.loop(0, early)
        def _(m):
            project(m)

    for k in range(1, n_obs):
        slab = ofull.at[p, :, cols(peers[k])]
        remote(sel, slab, o_send.at[k], o_recv.at[p, peers[k]], p, peers[k], z).wait_recv()
        forward(k).start()
    own_sel.wait()
    for k in range(n_obs):
        slab = ofull.at[1 - p, :, cols(peers[k])]
        remote(
            slab, slab, f_send.at[k], o_recv.at[1 - p, peers[k]], 1 - p, o, z
        ).wait_recv()

    w_copies[1].wait()
    w_copies[2].wait()

    @pl.loop(0, 2)
    def _(h):
        normed = rms_round(ofull[h], obs_gain[...])
        here = pl.ds(pl.multiple_of(h * half_rows, half_rows), half_rows)
        keys[here, :] = jnp.dot(normed, wk[...], preferred_element_type=F32).astype(BF16)
        vals[here, :] = jnp.dot(normed, wv[...], preferred_element_type=F32).astype(BF16)

    w_copies[3].wait()

    def piece_copy(m, k):
        return remote(
            pbuf.at[peers[k], rows(m), :], rbuf.at[o, rows(m), :],
            r_send.at[m, k], r_recv.at[m, o], p, peers[k], z,
        )

    def x1_copy(m, k):
        return remote(
            x1.at[rows(m), :], xbuf.at[rows(m), cols(o)],
            x_send.at[micro + m, k], x_recv.at[m, o], 1, peers[k], z,
        )

    def attend(m):
        row_bias = bias[pl.ds(m, 1), :]
        for h in range(heads):
            head = slice(h * HS, (h + 1) * HS)
            scores = lax.dot_general(
                queries[rows(m), head], keys[:, head], (((1,), (1,)), ((), ())),
                preferred_element_type=F32,
            )
            scores = scores + row_bias
            weights = jnp.exp(scores - jnp.max(scores, axis=-1, keepdims=True))
            total = jnp.sum(weights, axis=-1, keepdims=True)
            mixed = jnp.dot(weights.astype(BF16), vals[:, head], preferred_element_type=F32)
            context[:, head] = (mixed / total).astype(BF16)
        for k in list(range(1, n_obs)) + [0]:
            pbuf[peers[k], rows(m), :] = jnp.dot(
                context[...], wo[:, cols(peers[k])], preferred_element_type=F32
            ).astype(BF16)
            if k:
                piece_copy(m, k).start()

    def finish(m):
        for k in range(1, n_obs):
            remote(
                pbuf.at[peers[k], rows(m), :], rbuf.at[peers[k], rows(m), :],
                r_send.at[m, k], r_recv.at[m, peers[k]], p, peers[k], z,
            ).wait_recv()
        head_total = pbuf[o, rows(m), :].astype(F32)
        for k in range(1, n_obs):
            head_total = head_total + rbuf[peers[k], rows(m), :].astype(F32)
        result = (xbuf[rows(m), cols(o)].astype(F32) + head_total).astype(BF16)
        out[rows(m), :] = result

        @pl.when(p == 0)
        def _():
            x1[rows(m), :] = result
            for k in range(n_obs):
                x1_copy(m, (k + 1) % n_obs).start()

    @pl.loop(0, micro + 1)
    def _(t):
        @pl.when(t < micro)
        def _():
            @pl.when(p == 1)
            def _():
                remote(
                    x1.at[rows(t), :], xbuf.at[rows(t), cols(o)],
                    x_send.at[t, 0], x_recv.at[t, o], 0, o, z,
                ).wait_recv()

            @pl.when((p == 1) | (t >= early))
            def _():
                project(t)

            attend(t)

        @pl.when(t > 0)
        def _():
            finish(t - 1)

    for k in range(1, n_patch):
        wish_copy(k).wait_send()
        z_copy(k).wait_send()
    for k in range(n_obs):
        sel_copy(k).wait_send()
        if k:
            forward(k).wait_send()

    @pl.loop(0, micro)
    def _(m):
        for k in range(1, n_obs):
            piece_copy(m, k).wait_send()

        @pl.when(p == 0)
        def _():
            for k in range(1, n_obs):
                patch_copy(m, k).wait_send()
            for k in range(n_obs):
                x1_copy(m, k).wait_send()


def on_device(
    n_obs,
    n_patch,
    patch_tokens,
    obs_tokens,
    footprint,
    list_counts,
    footprint_bias,
    w_query,
    w_key,
    w_value,
    w_out,
    patch_gain,
    obs_gain,
):
    row_count, feat = patch_tokens.shape
    width = feat * n_obs
    head_width = w_query.shape[2]
    range_blocks = obs_tokens.shape[0] // BLK
    micro = row_count // BLK
    half_rows = n_patch * HALF
    hbm = pl.BlockSpec(memory_space=pltpu.MemorySpace.HBM)
    vmem = pl.BlockSpec(memory_space=pltpu.VMEM)
    dma = pltpu.SemaphoreType.DMA
    result = pl.pallas_call(
        functools.partial(kernel, n_obs, n_patch),
        out_shape=jax.ShapeDtypeStruct((row_count, feat), BF16),
        in_specs=[hbm, hbm, hbm, pl.BlockSpec(memory_space=pltpu.SMEM)] + [hbm] * 7,
        out_specs=vmem,
        scratch_shapes=[
            pltpu.VMEM(footprint.shape, jnp.int32),
            pltpu.VMEM(footprint_bias.shape, F32),
            pltpu.VMEM((1, width), F32),
            pltpu.VMEM((1, width), F32),
            pltpu.VMEM((width, head_width), BF16),
            pltpu.VMEM((width, head_width), BF16),
            pltpu.VMEM((width, head_width), BF16),
            pltpu.VMEM((head_width, width), BF16),
            pltpu.VMEM((row_count, width), BF16),
            pltpu.VMEM((range_blocks, HALF, feat), BF16),
            pltpu.VMEM((n_patch, HALF, feat), BF16),
            pltpu.VMEM((n_patch, 8, 128), F32),
            pltpu.VMEM((n_patch, 8, 128), F32),
            pltpu.VMEM((half_rows, feat), BF16),
            pltpu.VMEM((2, half_rows, width), BF16),
            pltpu.VMEM((2 * half_rows, head_width), BF16),
            pltpu.VMEM((2 * half_rows, head_width), BF16),
            pltpu.VMEM((row_count, head_width), BF16),
            pltpu.VMEM((BLK, head_width), BF16),
            pltpu.VMEM((n_obs, row_count, feat), BF16),
            pltpu.VMEM((n_obs, row_count, feat), BF16),
            pltpu.VMEM((row_count, feat), BF16),
            pltpu.VMEM((micro, 2 * half_rows), F32),
            dma((8,)),
            dma((3,)),
            dma((n_patch,)),
            dma((n_patch,)),
            dma((n_patch,)),
            dma((n_patch,)),
            dma((n_obs,)),
            dma((2, n_obs)),
            dma((n_obs,)),
            dma((2 * micro, n_obs)),
            dma((micro, n_obs)),
            dma((micro, n_obs)),
            dma((micro, n_obs)),
        ],
        compiler_params=pltpu.CompilerParams(
            collective_id=0, has_side_effects=True, vmem_limit_bytes=62 * 1024 * 1024
        ),
    )(
        patch_tokens,
        obs_tokens.reshape(range_blocks, 2, HALF, feat),
        footprint,
        list_counts,
        footprint_bias,
        w_query[0],
        w_key[0],
        w_value[0],
        w_out[0],
        patch_gain,
        obs_gain,
    )
    return result[None]


def solution(mesh):
    in_specs = (
        P("patch", "obs"),
        P("patch", "obs"),
        P("patch", None),
        P("patch"),
        P("patch", None),
        P("pipe", None, "obs"),
        P("pipe", None, "obs"),
        P("pipe", None, "obs"),
        P("pipe", "obs", None),
        P("pipe", None),
        P("pipe", None),
    )
    out_specs = P("pipe", "patch", "obs")
    return jax.shard_map(
        functools.partial(on_device, mesh.shape["obs"], mesh.shape["patch"]),
        mesh=mesh, in_specs=in_specs, out_specs=out_specs, check_vma=False,
    )
```

```python
import functools
import jax
import jax.numpy as jnp
from jax import lax
from jax.experimental import pallas as pl
from jax.experimental.pallas import tpu as pltpu
from jax.sharding import PartitionSpec as P

HS = 128
BLK = 128
HALF = BLK // 2
EPS = 1e-05
NEG = -1e30
F32 = jnp.float32
BF16 = jnp.bfloat16


def rms_round(values, gain):
    widened = values.astype(F32)
    scaled = widened * lax.rsqrt(jnp.mean(widened * widened, axis=-1, keepdims=True) + EPS)
    return (scaled * gain).astype(BF16)


def remote(src, dst, send_sem, recv_sem, pipe, obs, patch):
    return pltpu.make_async_remote_copy(
        src_ref=src,
        dst_ref=dst,
        send_sem=send_sem,
        recv_sem=recv_sem,
        device_id={"pipe": pipe, "obs": obs, "patch": patch},
        device_id_type=pl.DeviceIdType.MESH,
    )


def kernel(
    n_obs,
    n_patch,
    patch_hbm,
    obs_hbm,
    footprint_hbm,
    counts,
    slot_bias_hbm,
    wq_hbm,
    wk_hbm,
    wv_hbm,
    wo_hbm,
    patch_gain_hbm,
    obs_gain_hbm,
    out,
    footprint,
    slot_bias,
    patch_gain,
    obs_gain,
    wq,
    wk,
    wv,
    wo,
    xbuf,
    obs_own,
    zout,
    wish,
    asked,
    sel,
    ofull,
    keys,
    vals,
    queries,
    context,
    pbuf,
    rbuf,
    x1,
    bias,
    w_sem,
    own_sem,
    a_send,
    a_recv,
    z_send,
    z_recv,
    o_send,
    o_recv,
    f_send,
    x_send,
    x_recv,
    r_send,
    r_recv,
    xd_send,
    xd_recv,
    od_send,
    od_recv,
):
    p = lax.axis_index("pipe")
    o = lax.axis_index("obs")
    z = lax.axis_index("patch")
    rows_total, feat = out.shape
    micro = rows_total // BLK
    heads = wq.shape[1] // HS
    range_blocks = obs_own.shape[0]
    half_rows = sel.shape[0]
    relay = n_obs == 4
    if relay:
        side = o + 1 - 2 * lax.rem(o, 2)
        peers = [o, side, lax.rem(o + 2, 4), lax.rem(side + 2, 4)]
        direct = [1, 2]
    else:
        peers = [lax.rem(o + k, n_obs) for k in range(n_obs)]
        direct = list(range(1, n_obs))
    zpeers = [lax.rem(z + k, n_patch) for k in range(n_patch)]

    def cols(index):
        return pl.ds(pl.multiple_of(index * feat, feat), feat)

    def rows(index):
        return pl.ds(pl.multiple_of(index * BLK, BLK), BLK)

    barrier = pltpu.get_barrier_semaphore()
    for k in range(n_obs):
        pl.semaphore_signal(
            barrier, inc=1, device_id={"pipe": 1 - p, "obs": peers[k], "patch": z},
            device_id_type=pl.DeviceIdType.MESH,
        )
        if k:
            pl.semaphore_signal(
                barrier, inc=1, device_id={"pipe": p, "obs": peers[k], "patch": z},
                device_id_type=pl.DeviceIdType.MESH,
            )
    for k in range(1, n_patch):
        pl.semaphore_signal(
            barrier, inc=1, device_id={"pipe": p, "obs": o, "patch": zpeers[k]},
            device_id_type=pl.DeviceIdType.MESH,
        )
    small_copies = [
        pltpu.make_async_copy(src, dst, w_sem.at[4 + i])
        for i, (src, dst) in enumerate(
            (
                (footprint_hbm, footprint),
                (slot_bias_hbm, slot_bias),
                (patch_gain_hbm, patch_gain),
                (obs_gain_hbm, obs_gain),
            )
        )
    ]
    for copy in small_copies:
        copy.start()
    own_obs = pltpu.make_async_copy(obs_hbm.at[:, p], obs_own, own_sem.at[0])
    own_obs.start()
    own_patch = pltpu.make_async_copy(patch_hbm, xbuf.at[:, cols(o)], own_sem.at[1])

    @pl.when(p == 0)
    def _():
        own_patch.start()

    w_copies = [
        pltpu.make_async_copy(src, dst, w_sem.at[i])
        for i, (src, dst) in enumerate(
            ((wq_hbm, wq), (wk_hbm, wk), (wv_hbm, wv), (wo_hbm, wo))
        )
    ]
    for copy in w_copies:
        copy.start()
    small_copies[0].wait()
    small_copies[1].wait()
    listed = footprint[...].astype(F32)
    slots = lax.broadcasted_iota(jnp.int32, listed.shape, 1)
    row = lax.broadcasted_iota(jnp.int32, listed.shape, 0)
    live = jnp.zeros(listed.shape, jnp.int32)
    for b in range(listed.shape[0]):
        live = jnp.where(row == b, counts[b], live)
    alive = slots < live
    added = slot_bias[...]
    col = lax.broadcasted_iota(jnp.int32, bias.shape, 1)
    source = lax.rem(lax.div(col, HALF), n_patch)
    full_bias = jnp.full(bias.shape, NEG, F32)
    for zz in range(n_patch):
        low = zz * range_blocks
        match = alive & (listed >= float(low)) & (listed < float(low + range_blocks))
        one = jnp.max(jnp.where(match, added, NEG), axis=1, keepdims=True)
        full_bias = jnp.where(source == zz, one, full_bias)
        which = jnp.max(jnp.where(match, listed - float(low), 0.0), axis=1, keepdims=True)
        wish[zz] = jnp.broadcast_to(jnp.max(which, axis=0, keepdims=True), wish.shape[1:])
    bias[...] = full_bias

    pl.semaphore_wait(barrier, 2 * n_obs - 1 + n_patch - 1)

    def wish_copy(k):
        return remote(
            wish.at[zpeers[k]], asked.at[z], a_send.at[k], a_recv.at[z], p, o, zpeers[k]
        )

    def z_place(index):
        return pl.ds(pl.multiple_of(index * HALF, HALF), HALF)

    def z_copy(k):
        return remote(
            zout.at[k], sel.at[z_place(z), :], z_send.at[k], z_recv.at[z], p, o, zpeers[k]
        )

    def patch_copy(m, k):
        return remote(
            patch_hbm.at[rows(m), :], xbuf.at[rows(m), cols(o)],
            x_send.at[m, k], x_recv.at[m, o], 0, peers[k], z,
        )

    def pick(which):
        which = jnp.broadcast_to(which[0:1, 0:1], obs_own.shape[1:])
        picked = obs_own[0].astype(F32)
        for k in range(1, range_blocks):
            picked = jnp.where(which == float(k), obs_own[k].astype(F32), picked)
        return picked.astype(BF16)

    early = micro - 1
    for k in range(1, n_patch):
        wish_copy(k).start()

    @pl.when(p == 0)
    def _():
        @pl.loop(0, early)
        def _(m):
            for k in direct:
                patch_copy(m, k).start()

    own_obs.wait()
    sel[z_place(z), :] = pick(wish[z])
    for k in range(1, n_patch):
        remote(
            wish.at[zpeers[k]], asked.at[zpeers[k]], a_send.at[k], a_recv.at[zpeers[k]],
            p, o, zpeers[k],
        ).wait_recv()
        zout[k] = pick(asked[zpeers[k]])
        z_copy(k).start()
    for k in range(1, n_patch):
        remote(
            zout.at[k], sel.at[z_place(zpeers[k]), :], z_send.at[k], z_recv.at[zpeers[k]],
            p, o, zpeers[k],
        ).wait_recv()

    def sel_copy(k):
        if k == 0:
            return remote(
                sel, ofull.at[p, :, cols(o)], o_send.at[0], o_recv.at[p, o], 1 - p, o, z
            )
        return remote(
            sel, ofull.at[p, :, cols(o)], o_send.at[k], o_recv.at[p, o], p, peers[k], z
        )

    def forward(k):
        slab = ofull.at[p, :, cols(peers[k])]
        return remote(
            slab, slab, f_send.at[k], o_recv.at[p, peers[k]], 1 - p, o, z
        )

    for k in direct:
        sel_copy(k).start()
    sel_copy(0).start()
    own_sel = pltpu.make_async_copy(sel, ofull.at[p, :, cols(o)], own_sem.at[2])
    own_sel.start()

    @pl.when(p == 0)
    def _():
        @pl.loop(early, micro)
        def _(m):
            for k in direct:
                patch_copy(m, k).start()


    w_copies[0].wait()
    small_copies[2].wait()
    small_copies[3].wait()
    score_scale = HS ** (-0.5)

    def half_slab(m, k, column):
        start = pl.multiple_of(m * BLK + (k - 1) * HALF, HALF)
        return xbuf.at[pl.ds(start, HALF), cols(column)]

    def pass_x(m, k):
        slab = half_slab(m, k, peers[k])
        return remote(
            slab, slab, xd_send.at[m, k - 1], xd_recv.at[m, k - 1], p, peers[3 - k], z
        )

    def arrive_x(m):
        for k in direct:
            slab = xbuf.at[rows(m), cols(peers[k])]
            remote(
                slab, slab, x_send.at[m, k], x_recv.at[m, peers[k]], p, peers[k], z
            ).wait_recv()
            if relay:
                pass_x(m, k).start()

    def pass_o(k):
        part = half_rows // 2
        slab = ofull.at[p, (k - 1) * part : k * part, cols(peers[k])]
        return remote(slab, slab, od_send.at[k - 1], od_recv.at[k - 1], p, peers[3 - k], z)

    def project(m):
        if relay:
            for k in direct:
                slab = half_slab(m, k, peers[3])
                remote(
                    slab, slab, xd_send.at[m, k - 1], xd_recv.at[m, k - 1], p, peers[k], z
                ).wait_recv()
        normed = rms_round(xbuf[rows(m), :], patch_gain[...])
        queries[rows(m), :] = (
            jnp.dot(normed, wq[...], preferred_element_type=F32) * score_scale
        ).astype(BF16)

    @pl.when(p == 0)
    def _():
        own_patch.wait()

        @pl.loop(0, early)
        def _(m):
            arrive_x(m)

    def arrive_o():
        for k in direct:
            slab = ofull.at[p, :, cols(peers[k])]
            remote(
                sel, slab, o_send.at[k], o_recv.at[p, peers[k]], p, peers[k], z
            ).wait_recv()
            if relay:
                pass_o(k).start()
            forward(k).start()

    arrive_o()

    @pl.when(p == 0)
    def _():
        @pl.loop(0, early)
        def _(m):
            project(m)

    if relay:
        for k in direct:
            part = half_rows // 2
            slab = ofull.at[p, (k - 1) * part : k * part, cols(peers[3])]
            remote(
                slab, slab, od_send.at[k - 1], od_recv.at[k - 1], p, peers[k], z
            ).wait_recv()
        forward(3).start()

    @pl.when(p == 0)
    def _():
        @pl.loop(early, micro)
        def _(m):
            arrive_x(m)

    own_sel.wait()
    for k in range(n_obs):
        slab = ofull.at[1 - p, :, cols(peers[k])]
        remote(
            slab, slab, f_send.at[k], o_recv.at[1 - p, peers[k]], 1 - p, o, z
        ).wait_recv()

    w_copies[1].wait()
    w_copies[2].wait()

    @pl.loop(0, 2)
    def _(h):
        normed = rms_round(ofull[h], obs_gain[...])
        here = pl.ds(pl.multiple_of(h * half_rows, half_rows), half_rows)
        keys[here, :] = jnp.dot(normed, wk[...], preferred_element_type=F32).astype(BF16)
        vals[here, :] = jnp.dot(normed, wv[...], preferred_element_type=F32).astype(BF16)

    w_copies[3].wait()

    def piece_copy(m, k):
        return remote(
            pbuf.at[peers[k], rows(m), :], rbuf.at[o, rows(m), :],
            r_send.at[m, k], r_recv.at[m, o], p, peers[k], z,
        )

    def x1_copy(m, k):
        return remote(
            x1.at[rows(m), :], xbuf.at[rows(m), cols(o)],
            x_send.at[micro + m, k], x_recv.at[m, o], 1, peers[k], z,
        )

    def attend(m):
        row_bias = bias[pl.ds(m, 1), :]
        for h in range(heads):
            head = slice(h * HS, (h + 1) * HS)
            scores = lax.dot_general(
                queries[rows(m), head], keys[:, head], (((1,), (1,)), ((), ())),
                preferred_element_type=F32,
            )
            scores = scores + row_bias
            weights = jnp.exp(scores - jnp.max(scores, axis=-1, keepdims=True))
            total = jnp.sum(weights, axis=-1, keepdims=True)
            mixed = jnp.dot(weights.astype(BF16), vals[:, head], preferred_element_type=F32)
            context[:, head] = (mixed / total).astype(BF16)
        for k in list(range(n_obs - 1, 0, -1)) + [0]:
            pbuf[peers[k], rows(m), :] = jnp.dot(
                context[...], wo[:, cols(peers[k])], preferred_element_type=F32
            ).astype(BF16)
            if k:
                piece_copy(m, k).start()

    def finish(m):
        for k in range(1, n_obs):
            remote(
                pbuf.at[peers[k], rows(m), :], rbuf.at[peers[k], rows(m), :],
                r_send.at[m, k], r_recv.at[m, peers[k]], p, peers[k], z,
            ).wait_recv()
        head_total = pbuf[o, rows(m), :].astype(F32)
        for k in range(1, n_obs):
            head_total = head_total + rbuf[peers[k], rows(m), :].astype(F32)
        result = (xbuf[rows(m), cols(o)].astype(F32) + head_total).astype(BF16)
        out[rows(m), :] = result

        @pl.when(p == 0)
        def _():
            x1[rows(m), :] = result
            for k in direct + [0]:
                x1_copy(m, k).start()

    @pl.loop(0, micro + 1)
    def _(t):
        @pl.when(t < micro)
        def _():
            @pl.when(p == 1)
            def _():
                remote(
                    x1.at[rows(t), :], xbuf.at[rows(t), cols(o)],
                    x_send.at[t, 0], x_recv.at[t, o], 0, o, z,
                ).wait_recv()
                arrive_x(t)

            @pl.when((p == 1) | (t >= early))
            def _():
                project(t)

            attend(t)

        @pl.when(t > 0)
        def _():
            finish(t - 1)

    for k in range(1, n_patch):
        wish_copy(k).wait_send()
        z_copy(k).wait_send()
    for k in [0] + direct:
        sel_copy(k).wait_send()
    for k in range(1, n_obs):
        forward(k).wait_send()
    if relay:
        for k in direct:
            pass_o(k).wait_send()

    @pl.loop(0, micro)
    def _(m):
        for k in range(1, n_obs):
            piece_copy(m, k).wait_send()
        if relay:
            for k in direct:
                pass_x(m, k).wait_send()

        @pl.when(p == 0)
        def _():
            for k in direct:
                patch_copy(m, k).wait_send()
            for k in [0] + direct:
                x1_copy(m, k).wait_send()


def on_device(
    n_obs,
    n_patch,
    patch_tokens,
    obs_tokens,
    footprint,
    list_counts,
    footprint_bias,
    w_query,
    w_key,
    w_value,
    w_out,
    patch_gain,
    obs_gain,
):
    row_count, feat = patch_tokens.shape
    width = feat * n_obs
    head_width = w_query.shape[2]
    range_blocks = obs_tokens.shape[0] // BLK
    micro = row_count // BLK
    half_rows = n_patch * HALF
    hbm = pl.BlockSpec(memory_space=pltpu.MemorySpace.HBM)
    vmem = pl.BlockSpec(memory_space=pltpu.VMEM)
    dma = pltpu.SemaphoreType.DMA
    result = pl.pallas_call(
        functools.partial(kernel, n_obs, n_patch),
        out_shape=jax.ShapeDtypeStruct((row_count, feat), BF16),
        in_specs=[hbm, hbm, hbm, pl.BlockSpec(memory_space=pltpu.SMEM)] + [hbm] * 7,
        out_specs=vmem,
        scratch_shapes=[
            pltpu.VMEM(footprint.shape, jnp.int32),
            pltpu.VMEM(footprint_bias.shape, F32),
            pltpu.VMEM((1, width), F32),
            pltpu.VMEM((1, width), F32),
            pltpu.VMEM((width, head_width), BF16),
            pltpu.VMEM((width, head_width), BF16),
            pltpu.VMEM((width, head_width), BF16),
            pltpu.VMEM((head_width, width), BF16),
            pltpu.VMEM((row_count, width), BF16),
            pltpu.VMEM((range_blocks, HALF, feat), BF16),
            pltpu.VMEM((n_patch, HALF, feat), BF16),
            pltpu.VMEM((n_patch, 8, 128), F32),
            pltpu.VMEM((n_patch, 8, 128), F32),
            pltpu.VMEM((half_rows, feat), BF16),
            pltpu.VMEM((2, half_rows, width), BF16),
            pltpu.VMEM((2 * half_rows, head_width), BF16),
            pltpu.VMEM((2 * half_rows, head_width), BF16),
            pltpu.VMEM((row_count, head_width), BF16),
            pltpu.VMEM((BLK, head_width), BF16),
            pltpu.VMEM((n_obs, row_count, feat), BF16),
            pltpu.VMEM((n_obs, row_count, feat), BF16),
            pltpu.VMEM((row_count, feat), BF16),
            pltpu.VMEM((micro, 2 * half_rows), F32),
            dma((8,)),
            dma((3,)),
            dma((n_patch,)),
            dma((n_patch,)),
            dma((n_patch,)),
            dma((n_patch,)),
            dma((n_obs,)),
            dma((2, n_obs)),
            dma((n_obs,)),
            dma((2 * micro, n_obs)),
            dma((micro, n_obs)),
            dma((micro, n_obs)),
            dma((micro, n_obs)),
            dma((micro, 2)),
            dma((micro, 2)),
            dma((2,)),
            dma((2,)),
        ],
        compiler_params=pltpu.CompilerParams(
            collective_id=0, has_side_effects=True, vmem_limit_bytes=62 * 1024 * 1024
        ),
    )(
        patch_tokens,
        obs_tokens.reshape(range_blocks, 2, HALF, feat),
        footprint,
        list_counts,
        footprint_bias,
        w_query[0],
        w_key[0],
        w_value[0],
        w_out[0],
        patch_gain,
        obs_gain,
    )
    return result[None]


def solution(mesh):
    in_specs = (
        P("patch", "obs"),
        P("patch", "obs"),
        P("patch", None),
        P("patch"),
        P("patch", None),
        P("pipe", None, "obs"),
        P("pipe", None, "obs"),
        P("pipe", None, "obs"),
        P("pipe", "obs", None),
        P("pipe", None),
        P("pipe", None),
    )
    out_specs = P("pipe", "patch", "obs")
    return jax.shard_map(
        functools.partial(on_device, mesh.shape["obs"], mesh.shape["patch"]),
        mesh=mesh, in_specs=in_specs, out_specs=out_specs, check_vma=False,
    )
```

```python
import functools
import jax
import jax.numpy as jnp
from jax import lax
from jax.experimental import pallas as pl
from jax.experimental.pallas import tpu as pltpu
from jax.sharding import PartitionSpec as P

HS = 128
BLK = 128
HALF = BLK // 2
EPS = 1e-05
NEG = -1e30
F32 = jnp.float32
BF16 = jnp.bfloat16


def rms_round(values, gain):
    widened = values.astype(F32)
    scaled = widened * lax.rsqrt(jnp.mean(widened * widened, axis=-1, keepdims=True) + EPS)
    return (scaled * gain).astype(BF16)


def remote(src, dst, send_sem, recv_sem, pipe, obs, patch):
    return pltpu.make_async_remote_copy(
        src_ref=src,
        dst_ref=dst,
        send_sem=send_sem,
        recv_sem=recv_sem,
        device_id={"pipe": pipe, "obs": obs, "patch": patch},
        device_id_type=pl.DeviceIdType.MESH,
    )


def kernel(
    n_obs,
    n_patch,
    patch_hbm,
    obs_hbm,
    footprint_hbm,
    counts,
    slot_bias_hbm,
    wq_hbm,
    wk_hbm,
    wv_hbm,
    wo_hbm,
    patch_gain_hbm,
    obs_gain_hbm,
    out,
    footprint,
    slot_bias,
    patch_gain,
    obs_gain,
    wq,
    wk,
    wv,
    wo,
    xbuf,
    obs_own,
    zout,
    wish,
    asked,
    sel,
    ofull,
    keys,
    vals,
    queries,
    context,
    pbuf,
    rbuf,
    x1,
    bias,
    w_sem,
    own_sem,
    a_send,
    a_recv,
    z_send,
    z_recv,
    o_send,
    o_recv,
    f_send,
    x_send,
    x_recv,
    r_send,
    r_recv,
    xd_send,
    xd_recv,
    od_send,
    od_recv,
):
    p = lax.axis_index("pipe")
    o = lax.axis_index("obs")
    z = lax.axis_index("patch")
    rows_total, feat = out.shape
    micro = rows_total // BLK
    heads = wq.shape[1] // HS
    range_blocks = obs_own.shape[0]
    half_rows = sel.shape[0]
    relay = n_obs == 4
    if relay:
        side = o + 1 - 2 * lax.rem(o, 2)
        peers = [o, side, lax.rem(o + 2, 4), lax.rem(side + 2, 4)]
        direct = [1, 2]
    else:
        peers = [lax.rem(o + k, n_obs) for k in range(n_obs)]
        direct = list(range(1, n_obs))
    zpeers = [lax.rem(z + k, n_patch) for k in range(n_patch)]

    def cols(index):
        return pl.ds(pl.multiple_of(index * feat, feat), feat)

    def rows(index):
        return pl.ds(pl.multiple_of(index * BLK, BLK), BLK)

    barrier = pltpu.get_barrier_semaphore()
    for k in range(n_obs):
        pl.semaphore_signal(
            barrier, inc=1, device_id={"pipe": 1 - p, "obs": peers[k], "patch": z},
            device_id_type=pl.DeviceIdType.MESH,
        )
        if k:
            pl.semaphore_signal(
                barrier, inc=1, device_id={"pipe": p, "obs": peers[k], "patch": z},
                device_id_type=pl.DeviceIdType.MESH,
            )
    for k in range(1, n_patch):
        pl.semaphore_signal(
            barrier, inc=1, device_id={"pipe": p, "obs": o, "patch": zpeers[k]},
            device_id_type=pl.DeviceIdType.MESH,
        )
    small_copies = [
        pltpu.make_async_copy(src, dst, w_sem.at[4 + i])
        for i, (src, dst) in enumerate(
            (
                (footprint_hbm, footprint),
                (slot_bias_hbm, slot_bias),
                (patch_gain_hbm, patch_gain),
                (obs_gain_hbm, obs_gain),
            )
        )
    ]
    for copy in small_copies:
        copy.start()
    own_obs = pltpu.make_async_copy(obs_hbm.at[:, p], obs_own, own_sem.at[0])
    own_obs.start()
    own_patch = pltpu.make_async_copy(patch_hbm, xbuf.at[:, cols(o)], own_sem.at[1])

    @pl.when(p == 0)
    def _():
        own_patch.start()

    w_copies = [
        pltpu.make_async_copy(src, dst, w_sem.at[i])
        for i, (src, dst) in enumerate(
            ((wq_hbm, wq), (wk_hbm, wk), (wv_hbm, wv), (wo_hbm, wo))
        )
    ]
    for copy in w_copies:
        copy.start()
    small_copies[0].wait()
    small_copies[1].wait()
    listed = footprint[...].astype(F32)
    slots = lax.broadcasted_iota(jnp.int32, listed.shape, 1)
    row = lax.broadcasted_iota(jnp.int32, listed.shape, 0)
    live = jnp.zeros(listed.shape, jnp.int32)
    for b in range(listed.shape[0]):
        live = jnp.where(row == b, counts[b], live)
    alive = slots < live
    added = slot_bias[...]
    col = lax.broadcasted_iota(jnp.int32, bias.shape, 1)
    source = lax.rem(lax.div(col, HALF), n_patch)
    full_bias = jnp.full(bias.shape, NEG, F32)
    for zz in range(n_patch):
        low = zz * range_blocks
        match = alive & (listed >= float(low)) & (listed < float(low + range_blocks))
        one = jnp.max(jnp.where(match, added, NEG), axis=1, keepdims=True)
        full_bias = jnp.where(source == zz, one, full_bias)
        which = jnp.max(jnp.where(match, listed - float(low), 0.0), axis=1, keepdims=True)
        wish[zz] = jnp.broadcast_to(jnp.max(which, axis=0, keepdims=True), wish.shape[1:])
    bias[...] = full_bias

    pl.semaphore_wait(barrier, 2 * n_obs - 1 + n_patch - 1)

    def wish_copy(k):
        return remote(
            wish.at[zpeers[k]], asked.at[z], a_send.at[k], a_recv.at[z], p, o, zpeers[k]
        )

    def z_place(index):
        return pl.ds(pl.multiple_of(index * HALF, HALF), HALF)

    def z_copy(k):
        return remote(
            zout.at[k], sel.at[z_place(z), :], z_send.at[k], z_recv.at[z], p, o, zpeers[k]
        )

    def patch_copy(m, k):
        return remote(
            patch_hbm.at[rows(m), :], xbuf.at[rows(m), cols(o)],
            x_send.at[m, k], x_recv.at[m, o], 0, peers[k], z,
        )

    def pick(which):
        which = jnp.broadcast_to(which[0:1, 0:1], obs_own.shape[1:])
        picked = obs_own[0].astype(F32)
        for k in range(1, range_blocks):
            picked = jnp.where(which == float(k), obs_own[k].astype(F32), picked)
        return picked.astype(BF16)

    early = micro - 1
    for k in range(1, n_patch):
        wish_copy(k).start()

    @pl.when(p == 0)
    def _():
        @pl.loop(0, early)
        def _(m):
            for k in direct:
                patch_copy(m, k).start()

    own_obs.wait()
    sel[z_place(z), :] = pick(wish[z])
    for k in range(1, n_patch):
        remote(
            wish.at[zpeers[k]], asked.at[zpeers[k]], a_send.at[k], a_recv.at[zpeers[k]],
            p, o, zpeers[k],
        ).wait_recv()
        zout[k] = pick(asked[zpeers[k]])
        z_copy(k).start()
    for k in range(1, n_patch):
        remote(
            zout.at[k], sel.at[z_place(zpeers[k]), :], z_send.at[k], z_recv.at[zpeers[k]],
            p, o, zpeers[k],
        ).wait_recv()

    def sel_copy(k):
        if k == 0:
            return remote(
                sel, ofull.at[p, :, cols(o)], o_send.at[0], o_recv.at[p, o], 1 - p, o, z
            )
        return remote(
            sel, ofull.at[p, :, cols(o)], o_send.at[k], o_recv.at[p, o], p, peers[k], z
        )

    def forward(k):
        slab = ofull.at[p, :, cols(peers[k])]
        return remote(
            slab, slab, f_send.at[k], o_recv.at[p, peers[k]], 1 - p, o, z
        )

    for k in direct:
        sel_copy(k).start()
    sel_copy(0).start()
    own_sel = pltpu.make_async_copy(sel, ofull.at[p, :, cols(o)], own_sem.at[2])
    own_sel.start()

    @pl.when(p == 0)
    def _():
        @pl.loop(early, micro)
        def _(m):
            for k in direct:
                patch_copy(m, k).start()


    w_copies[0].wait()
    small_copies[2].wait()
    small_copies[3].wait()
    score_scale = HS ** (-0.5)

    def half_slab(m, k, column):
        start = pl.multiple_of(m * BLK + (k - 1) * HALF, HALF)
        return xbuf.at[pl.ds(start, HALF), cols(column)]

    def pass_x(m, k):
        slab = half_slab(m, k, peers[k])
        return remote(
            slab, slab, xd_send.at[m, k - 1], xd_recv.at[m, k - 1], p, peers[3 - k], z
        )

    def arrive_x(m):
        for k in direct:
            slab = xbuf.at[rows(m), cols(peers[k])]
            remote(
                slab, slab, x_send.at[m, k], x_recv.at[m, peers[k]], p, peers[k], z
            ).wait_recv()
            if relay:
                pass_x(m, k).start()

    def pass_o(k):
        part = half_rows // 2
        slab = ofull.at[p, (k - 1) * part : k * part, cols(peers[k])]
        return remote(slab, slab, od_send.at[k - 1], od_recv.at[k - 1], p, peers[3 - k], z)

    def arrive_diagonal(m):
        if relay:
            for k in direct:
                slab = half_slab(m, k, peers[3])
                remote(
                    slab, slab, xd_send.at[m, k - 1], xd_recv.at[m, k - 1], p, peers[k], z
                ).wait_recv()

    def project(m):
        normed = rms_round(xbuf[rows(m), :], patch_gain[...])
        queries[rows(m), :] = (
            jnp.dot(normed, wq[...], preferred_element_type=F32) * score_scale
        ).astype(BF16)

    @pl.when(p == 0)
    def _():
        own_patch.wait()

        @pl.loop(0, early)
        def _(m):
            arrive_x(m)

    def arrive_o():
        for k in direct:
            slab = ofull.at[p, :, cols(peers[k])]
            remote(
                sel, slab, o_send.at[k], o_recv.at[p, peers[k]], p, peers[k], z
            ).wait_recv()
            if relay:
                pass_o(k).start()
            forward(k).start()

    arrive_o()

    @pl.when(p == 0)
    def _():
        @pl.loop(0, early)
        def _(m):
            arrive_diagonal(m)
            project(m)

    if relay:
        for k in direct:
            part = half_rows // 2
            slab = ofull.at[p, (k - 1) * part : k * part, cols(peers[3])]
            remote(
                slab, slab, od_send.at[k - 1], od_recv.at[k - 1], p, peers[k], z
            ).wait_recv()
        forward(3).start()

    @pl.when(p == 0)
    def _():
        @pl.loop(early, micro)
        def _(m):
            arrive_x(m)

    own_sel.wait()
    for k in range(n_obs):
        slab = ofull.at[1 - p, :, cols(peers[k])]
        remote(
            slab, slab, f_send.at[k], o_recv.at[1 - p, peers[k]], 1 - p, o, z
        ).wait_recv()

    w_copies[1].wait()
    w_copies[2].wait()

    @pl.loop(0, 2)
    def _(h):
        normed = rms_round(ofull[h], obs_gain[...])
        here = pl.ds(pl.multiple_of(h * half_rows, half_rows), half_rows)
        keys[here, :] = jnp.dot(normed, wk[...], preferred_element_type=F32).astype(BF16)
        vals[here, :] = jnp.dot(normed, wv[...], preferred_element_type=F32).astype(BF16)

    w_copies[3].wait()

    def piece_copy(m, k):
        return remote(
            pbuf.at[peers[k], rows(m), :], rbuf.at[o, rows(m), :],
            r_send.at[m, k], r_recv.at[m, o], p, peers[k], z,
        )

    def x1_copy(m, k):
        return remote(
            x1.at[rows(m), :], xbuf.at[rows(m), cols(o)],
            x_send.at[micro + m, k], x_recv.at[m, o], 1, peers[k], z,
        )

    def attend(m):
        row_bias = bias[pl.ds(m, 1), :]
        for h in range(heads):
            head = slice(h * HS, (h + 1) * HS)
            scores = lax.dot_general(
                queries[rows(m), head], keys[:, head], (((1,), (1,)), ((), ())),
                preferred_element_type=F32,
            )
            scores = scores + row_bias
            weights = jnp.exp(scores - jnp.max(scores, axis=-1, keepdims=True))
            total = jnp.sum(weights, axis=-1, keepdims=True)
            mixed = jnp.dot(weights.astype(BF16), vals[:, head], preferred_element_type=F32)
            context[:, head] = (mixed / total).astype(BF16)
        for k in list(range(n_obs - 1, 0, -1)) + [0]:
            pbuf[peers[k], rows(m), :] = jnp.dot(
                context[...], wo[:, cols(peers[k])], preferred_element_type=F32
            ).astype(BF16)
            if k:
                piece_copy(m, k).start()

    def finish(m):
        for k in range(1, n_obs):
            remote(
                pbuf.at[peers[k], rows(m), :], rbuf.at[peers[k], rows(m), :],
                r_send.at[m, k], r_recv.at[m, peers[k]], p, peers[k], z,
            ).wait_recv()
        head_total = pbuf[o, rows(m), :].astype(F32)
        for k in range(1, n_obs):
            head_total = head_total + rbuf[peers[k], rows(m), :].astype(F32)
        result = (xbuf[rows(m), cols(o)].astype(F32) + head_total).astype(BF16)
        out[rows(m), :] = result

        @pl.when(p == 0)
        def _():
            x1[rows(m), :] = result
            for k in list(range(n_obs - 1, 0, -1)) + [0]:
                x1_copy(m, k).start()

    @pl.loop(0, micro + 1)
    def _(t):
        @pl.when(t < micro)
        def _():
            @pl.when(p == 1)
            def _():
                remote(
                    x1.at[rows(t), :], xbuf.at[rows(t), cols(o)],
                    x_send.at[t, 0], x_recv.at[t, o], 0, o, z,
                ).wait_recv()
                for k in range(1, n_obs):
                    slab = xbuf.at[rows(t), cols(peers[k])]
                    remote(
                        slab, slab, x_send.at[t, k], x_recv.at[t, peers[k]], p, peers[k], z
                    ).wait_recv()

            @pl.when((p == 0) & (t >= early))
            def _():
                arrive_diagonal(t)

            @pl.when((p == 1) | (t >= early))
            def _():
                project(t)

            attend(t)

        @pl.when(t > 0)
        def _():
            finish(t - 1)

    for k in range(1, n_patch):
        wish_copy(k).wait_send()
        z_copy(k).wait_send()
    for k in [0] + direct:
        sel_copy(k).wait_send()
    for k in range(1, n_obs):
        forward(k).wait_send()
    if relay:
        for k in direct:
            pass_o(k).wait_send()

    @pl.loop(0, micro)
    def _(m):
        for k in range(1, n_obs):
            piece_copy(m, k).wait_send()

        @pl.when(p == 0)
        def _():
            if relay:
                for k in direct:
                    pass_x(m, k).wait_send()
            for k in direct:
                patch_copy(m, k).wait_send()
            for k in range(n_obs):
                x1_copy(m, k).wait_send()


def on_device(
    n_obs,
    n_patch,
    patch_tokens,
    obs_tokens,
    footprint,
    list_counts,
    footprint_bias,
    w_query,
    w_key,
    w_value,
    w_out,
    patch_gain,
    obs_gain,
):
    row_count, feat = patch_tokens.shape
    width = feat * n_obs
    head_width = w_query.shape[2]
    range_blocks = obs_tokens.shape[0] // BLK
    micro = row_count // BLK
    half_rows = n_patch * HALF
    hbm = pl.BlockSpec(memory_space=pltpu.MemorySpace.HBM)
    vmem = pl.BlockSpec(memory_space=pltpu.VMEM)
    dma = pltpu.SemaphoreType.DMA
    result = pl.pallas_call(
        functools.partial(kernel, n_obs, n_patch),
        out_shape=jax.ShapeDtypeStruct((row_count, feat), BF16),
        in_specs=[hbm, hbm, hbm, pl.BlockSpec(memory_space=pltpu.SMEM)] + [hbm] * 7,
        out_specs=vmem,
        scratch_shapes=[
            pltpu.VMEM(footprint.shape, jnp.int32),
            pltpu.VMEM(footprint_bias.shape, F32),
            pltpu.VMEM((1, width), F32),
            pltpu.VMEM((1, width), F32),
            pltpu.VMEM((width, head_width), BF16),
            pltpu.VMEM((width, head_width), BF16),
            pltpu.VMEM((width, head_width), BF16),
            pltpu.VMEM((head_width, width), BF16),
            pltpu.VMEM((row_count, width), BF16),
            pltpu.VMEM((range_blocks, HALF, feat), BF16),
            pltpu.VMEM((n_patch, HALF, feat), BF16),
            pltpu.VMEM((n_patch, 8, 128), F32),
            pltpu.VMEM((n_patch, 8, 128), F32),
            pltpu.VMEM((half_rows, feat), BF16),
            pltpu.VMEM((2, half_rows, width), BF16),
            pltpu.VMEM((2 * half_rows, head_width), BF16),
            pltpu.VMEM((2 * half_rows, head_width), BF16),
            pltpu.VMEM((row_count, head_width), BF16),
            pltpu.VMEM((BLK, head_width), BF16),
            pltpu.VMEM((n_obs, row_count, feat), BF16),
            pltpu.VMEM((n_obs, row_count, feat), BF16),
            pltpu.VMEM((row_count, feat), BF16),
            pltpu.VMEM((micro, 2 * half_rows), F32),
            dma((8,)),
            dma((3,)),
            dma((n_patch,)),
            dma((n_patch,)),
            dma((n_patch,)),
            dma((n_patch,)),
            dma((n_obs,)),
            dma((2, n_obs)),
            dma((n_obs,)),
            dma((2 * micro, n_obs)),
            dma((micro, n_obs)),
            dma((micro, n_obs)),
            dma((micro, n_obs)),
            dma((micro, 2)),
            dma((micro, 2)),
            dma((2,)),
            dma((2,)),
        ],
        compiler_params=pltpu.CompilerParams(
            collective_id=0, has_side_effects=True, vmem_limit_bytes=62 * 1024 * 1024
        ),
    )(
        patch_tokens,
        obs_tokens.reshape(range_blocks, 2, HALF, feat),
        footprint,
        list_counts,
        footprint_bias,
        w_query[0],
        w_key[0],
        w_value[0],
        w_out[0],
        patch_gain,
        obs_gain,
    )
    return result[None]


def solution(mesh):
    in_specs = (
        P("patch", "obs"),
        P("patch", "obs"),
        P("patch", None),
        P("patch"),
        P("patch", None),
        P("pipe", None, "obs"),
        P("pipe", None, "obs"),
        P("pipe", None, "obs"),
        P("pipe", "obs", None),
        P("pipe", None),
        P("pipe", None),
    )
    out_specs = P("pipe", "patch", "obs")
    return jax.shard_map(
        functools.partial(on_device, mesh.shape["obs"], mesh.shape["patch"]),
        mesh=mesh, in_specs=in_specs, out_specs=out_specs, check_vma=False,
    )
```
